32 devices in a mesh: mpo: 4 (over y, core), blk: 8 (over z, x).
Axes of the slice: x: 2, y: 2, z: 4, core: 2. Of those that a mesh axis runs over, the one named last changes fastest.
Arguments:
- two_site: bfloat16 [64, 16, 128, 128], P('blk'), may hold values from -6 to 6
- left_env: bfloat16 [34, 64, 128, 128], P(None, 'blk'), may hold values from -0.5 to 0.5
- right_env: bfloat16 [34, 64, 128, 128], P(None, 'blk'), may hold values from -0.5 to 0.5
- mpo_terms: bfloat16 [32, 16, 16], P('mpo'), may hold values from -0.25 to 0.25
- term_left: int32 [32], P('mpo'), may hold values from 0 to 33
- term_right: int32 [32], P('mpo'), may hold values from 0 to 33
- shifts: int32 [16], replicated, may hold values from -1 to 1, as said below
- block_sizes: int32 [64], replicated, may hold values from 64 to 128, as said below
Outputs:
- applied: bfloat16 [64, 16, 128, 128], P('blk', 'mpo')
The draws below stay inside these ranges and needn't reach their ends.
Inputs may be any that keep to these rules, and one draw needn't show every extreme that they name: `shifts`: both -1 and 1 occur among the offsets. `block_sizes`: both 128 // 2 and 128 occur among the live dimensions.
All inputs are finite; a program needn't handle non-finite values.
Results may differ from the reference program's by a relative error of at most 0.0057.
Values may be sent and summed in bfloat16 or wider, within the bound.
No kernel may reach another device: no remote copies, remote signals or barrier semaphores. Data moves between devices by JAX's collectives and lax.ppermute only.
A program may use at most 128 MiB of HBM per device.

```python
import jax
import jax.numpy as jnp
from jax import lax

W = 34
P_SIZE = 16
DB = 128
SH = 1
NL = 64
NT = 32


def draw_shifts(key, part):
    values = jax.random.randint(jax.random.fold_in(key, 11), (P_SIZE,), -SH, SH + 1)
    order = jax.random.permutation(jax.random.fold_in(key, 12), P_SIZE)
    values = values.at[order[0]].set(-SH)
    values = values.at[order[1]].set(SH)
    return values.astype(jnp.int32)


def draw_block_sizes(key, part):
    values = jax.random.randint(jax.random.fold_in(key, 21), (NL,), DB // 2, DB + 1)
    order = jax.random.permutation(jax.random.fold_in(key, 22), NL)
    values = values.at[order[0]].set(DB // 2)
    values = values.at[order[1]].set(DB)
    return values.astype(jnp.int32)


def set_ends(values, own_key, least, largest):
    longest = values.shape.index(max(values.shape))
    spots = []
    for shift in (0, 1):
        where = [jax.random.randint(jax.random.fold_in(own_key, axis), (), 0, length) for axis, length in enumerate(values.shape)]
        where[longest] = (where[longest] + shift) % values.shape[longest]
        spots.append(tuple(where))
    return values.at[spots[0]].set(least).at[spots[1]].set(largest)


def block_scale(key, shape, split, least, top_value):
    factor_of, own = 1.0, jax.random.fold_in(key, 6)
    for position, shards_of in split:
        draws = jnp.exp(jax.random.uniform(jax.random.fold_in(own, position), (shards_of,), jnp.float32, least / len(split), top_value / len(split)))
        factor_of = factor_of * jnp.repeat(draws, shape[position] // shards_of).reshape([-1 if axis == position else 1 for axis in range(len(shape))])
    return factor_of


def normal_values(stream_key, extent, scale, most, pieces=(), kind=jnp.bfloat16):
    loudness = block_scale(stream_key, extent, pieces, -0.22, 0.18) if pieces else 1.0
    drawn = jax.random.normal(stream_key, extent, jnp.float32) * scale * loudness
    return jnp.minimum(jnp.maximum(drawn, -most), most).astype(kind)


def setup_inputs(seed: int = 0) -> dict:
    arg_keys = jax.random.split(jax.random.key(seed), 9)
    return {
        "two_site": normal_values(arg_keys[0], (NL, P_SIZE, DB, DB), 1.0, 6.0, ((0, 8),)),
        "left_env": normal_values(arg_keys[1], (W, NL, DB, DB), DB ** -0.5, 0.5, ((1, 8),)),
        "right_env": normal_values(arg_keys[2], (W, NL, DB, DB), DB ** -0.5, 0.5, ((1, 8),)),
        "mpo_terms": normal_values(arg_keys[3], (NT, P_SIZE, P_SIZE), (NT * P_SIZE) ** -0.5, 0.25, ((0, 4),)),
        "term_left": set_ends(jax.random.randint(arg_keys[4], (NT,), 0, W), jax.random.fold_in(arg_keys[4], 1), 0, W - 1).astype(jnp.int32),
        "term_right": set_ends(jax.random.randint(arg_keys[5], (NT,), 0, W), jax.random.fold_in(arg_keys[5], 1), 0, W - 1).astype(jnp.int32),
        "shifts": draw_shifts(jax.random.fold_in(arg_keys[8], 71), 0),
        "block_sizes": draw_block_sizes(jax.random.fold_in(arg_keys[8], 71), 0),
    }


def sector_mask(block_sizes, shifts, first, blocks, total, depth):
    rows_left = first + jnp.arange(blocks, dtype=jnp.int32)
    right_index = rows_left[:, None] + shifts[None, :]
    inside = (right_index >= 0) & (right_index < total)
    table = jnp.arange(total, dtype=jnp.int32)
    size_left = jnp.sum(jnp.where(rows_left[:, None] == table[None, :], block_sizes[None, :], 0), axis=1)
    size_right = jnp.sum(jnp.where(right_index[:, :, None] == table[None, None, :], block_sizes[None, None, :], 0), axis=2)
    lines = jnp.arange(depth, dtype=jnp.int32)
    keep_rows = lines[None, None, :, None] < size_left[:, None, None, None]
    keep_cols = lines[None, None, None, :] < size_right[:, :, None, None]
    return keep_rows & keep_cols & inside[:, :, None, None]


def reference(two_site, left_env, right_env, mpo_terms, term_left, term_right, shifts, block_sizes):
    mask = sector_mask(block_sizes, shifts, 0, NL, NL, DB)
    clean = jnp.where(mask, two_site, jnp.zeros_like(two_site))
    padded = jnp.pad(right_env, ((0, 0), (SH, SH), (0, 0), (0, 0)))
    starts = (shifts + SH).astype(jnp.int32)

    def one_term(summed, item):
        left_index, right_index, matrix = item
        left_block = lax.dynamic_index_in_dim(left_env, left_index, 0, keepdims=False)
        applied_left = jnp.einsum('bxy,bqyz->bqxz', left_block.astype(jnp.float32), clean.astype(jnp.float32), precision=lax.Precision.HIGHEST)
        applied_half = applied_left.astype(jnp.bfloat16)
        mixed = jnp.einsum('pq,bqxz->bpxz', matrix.astype(jnp.float32), applied_half.astype(jnp.float32), precision=lax.Precision.HIGHEST)
        mixed_half = mixed.astype(jnp.bfloat16)
        right_rows = lax.dynamic_index_in_dim(padded, right_index, 0, keepdims=False)
        gathered = jax.vmap(lambda begin: lax.dynamic_slice_in_dim(right_rows, begin, NL, 0))(starts)
        product = jnp.einsum('bpxz,pbzy->bpxy', mixed_half.astype(jnp.float32), gathered.astype(jnp.float32), precision=lax.Precision.HIGHEST)
        return summed + product, None

    summed, unused = lax.scan(one_term, jnp.zeros(two_site.shape, jnp.float32), (term_left, term_right, mpo_terms))
    return jnp.where(mask, summed, jnp.float32(0.0)).astype(jnp.bfloat16)
```

```python
import functools

import jax
import jax.numpy as jnp
from jax import lax
from jax.experimental import pallas as pl
from jax.experimental.pallas import tpu as pltpu
from jax.sharding import PartitionSpec as P

BF, F32, I32 = jnp.bfloat16, jnp.float32, jnp.int32
ROWS = 16
VMEM_LIMIT = 60 * 2**20


def dot(a, b):
    return jnp.dot(a, b, preferred_element_type=F32)


def iota(shape, axis):
    return lax.broadcasted_iota(I32, shape, axis)


def pack_kernel(left_ref, right_ref, terms_ref, packed_ref):
    terms, states, _ = terms_ref.shape
    packed_ref[...] = jnp.zeros_like(packed_ref)
    packed_ref[:, :, :states] = terms_ref[...]
    lane = iota((states, packed_ref.shape[2]), 1)
    for t in range(terms):
        row = packed_ref[t].astype(F32)
        row = jnp.where(lane == states, left_ref[t].astype(F32), row)
        row = jnp.where(lane == states + 1, right_ref[t].astype(F32), row)
        packed_ref[t] = row.astype(BF)


def gathered(mine, axis):
    count = lax.axis_size(axis)
    turns = [[(m, (m + turn) % count) for m in range(count)] for turn in range(1, count)]
    return jnp.stack([mine, *(lax.ppermute(mine, axis, pairs) for pairs in turns)])


def pack(term_left, term_right, mpo_terms):
    terms, states, _ = mpo_terms.shape
    smem = pl.BlockSpec(memory_space=pltpu.SMEM)
    vmem = pl.BlockSpec(memory_space=pltpu.VMEM)
    return pl.pallas_call(
        pack_kernel,
        out_shape=jax.ShapeDtypeStruct((terms, states, 128), BF),
        in_specs=[smem, smem, vmem],
        out_specs=vmem,
        name="pack_terms",
    )(term_left, term_right, mpo_terms)


def spread_terms(packed, spread, own, mine):
    terms, states, depth = packed.shape
    held, width = terms * own, states * ROWS
    row, col = iota((held, terms * states), 0), iota((held, terms * states), 1)
    pick = jnp.where(col == (row // own) * states + mine + row % own, 1.0, 0.0).astype(BF)
    wide = iota((depth, width), 0) == iota((depth, width), 1) // ROWS
    chosen = dot(pick, packed[...].reshape(terms * states, depth)).astype(BF)
    chosen = dot(chosen, jnp.where(wide, 1.0, 0.0).astype(BF))
    diagonal = iota((ROWS, width), 0) == iota((ROWS, width), 1) % ROWS
    for r in range(held):
        line = jnp.broadcast_to(chosen[r : r + 1, :], (ROWS, width))
        spread[r * ROWS : (r + 1) * ROWS, :] = jnp.where(diagonal, line, 0.0).astype(BF)


def block_kernel(edges, start, stop, own, total, *refs):
    refs = list(refs)
    shifts, sizes, packed = refs[:3]
    refs = refs[3:]
    first_call = start == 1 and not edges
    if not first_call:
        spread, _ = refs[:2]
        refs = refs[2:]
    two, left, right = refs[:3]
    refs = refs[3:]
    if edges:
        halo = refs[:4]
        refs = refs[4:]
    out = refs.pop(0)
    if first_call:
        spread = refs.pop(0)
    clean, lefts, rights, mixed, joined, result, wide, index, sems, out_sems = refs

    blocks, states, depth, _ = two.shape
    terms = packed.shape[0]
    bonds = left.shape[0]
    me = lax.axis_index("mpo")
    first = lax.axis_index("blk") * blocks
    mine = me * own

    if edges:
        count = 2
        half = halo[0].shape[0]
        core = lax.rem(me, 2)
        place = lambda n: n * (blocks - 1)
    else:
        count = stop - start
        place = lambda n: start + n

    def two_copy(n):
        return pltpu.make_async_copy(two.at[place(n)], clean.at[n], sems.at[0, n])

    def left_copy(n):
        return pltpu.make_async_copy(left.at[:, place(n)], lefts.at[n], sems.at[1, n])

    def right_copies(slot):
        if not edges:
            return [pltpu.make_async_copy(right.at[:, start - 1 + slot], rights.at[slot], sems.at[2, slot])]
        if slot in (0, 5):
            side = 0 if slot == 0 else 2
            return [
                pltpu.make_async_copy(
                    halo[side], rights.at[slot, pl.ds(core * half, half)], sems.at[2, slot]
                ),
                pltpu.make_async_copy(
                    halo[side + 1],
                    rights.at[slot, pl.ds((1 - core) * half, half)],
                    sems.at[2, slot + 1 if slot == 0 else slot + 2],
                ),
            ]
        block = slot - 1 if slot < 3 else blocks - 5 + slot
        return [pltpu.make_async_copy(right.at[:, block], rights.at[slot], sems.at[2, slot + 1])]

    def right_wait(slot):
        pltpu.make_async_copy(right.at[:, 0], rights.at[slot], sems.at[2, slot]).wait()

    two_copy(0).start()
    slots = 6 if edges else count + 2
    for n in range(count):
        news = ([0, 1, 2] if n == 0 else [3, 4, 5]) if edges else ([0, 1, 2] if n == 0 else [n + 2])
        for slot in news:
            for copy in right_copies(slot):
                copy.start()
        left_copy(n).start()
        if n + 1 < count:
            two_copy(n + 1).start()

    wide[...] = packed[:, 0, :].astype(F32).astype(I32)
    index_copy = pltpu.make_async_copy(wide, index, out_sems.at[count])
    index_copy.start()
    if first_call:
        spread_terms(packed, spread, own, mine)
    index_copy.wait()

    if edges:
        for slot in range(6):
            for copy in right_copies(slot):
                copy.wait()
    else:
        right_wait(0)
        right_wait(1)

    @pl.loop(0, count)
    def _(n):
        i = place(n)
        size = sizes[first + i]

        def width(p):
            j = first + i + shifts[p]
            return jnp.where((j >= 0) & (j < total), sizes[jnp.clip(j, 0, total - 1)], 0)

        two_copy(n).wait()
        keep_rows = jnp.where(iota((depth, depth), 0) < size, 1.0, 0.0).astype(BF)
        lane = iota((ROWS, depth), 1)
        for q in range(states):
            keep_cols = jnp.where(lane < width(q), 1.0, 0.0).astype(BF)
            block = clean[n, q].reshape(depth // ROWS, ROWS, depth) * keep_cols[None]
            clean[n, q] = block.reshape(depth, depth) * keep_rows

        for h in range(depth // (2 * ROWS)):
            spans = [slice((2 * h + u) * ROWS, (2 * h + u + 1) * ROWS) for u in range(2)]
            both = jnp.concatenate(
                [clean[n, :, s, :].reshape(states * ROWS, depth) for s in spans], axis=1
            )
            part = dot(spread[...], both).astype(BF).reshape(terms, own, ROWS, 2 * depth)
            for u in range(2):
                mixed[:, :, spans[u], :] = part[:, :, :, u * depth : (u + 1) * depth]

        if not edges:
            right_wait(n + 2)
        base = n * 3 + 1 if edges else n + 1
        slot_of = [base + shifts[mine + p] for p in range(own)]
        for t in range(terms):
            bond = index[t, states + 1]
            for p in range(own):
                joined[t, :, p * depth : (p + 1) * depth] = dot(
                    mixed[t, p], rights[slot_of[p], bond]
                ).astype(BF)

        left_copy(n).wait()
        row = jnp.concatenate([lefts[n, index[t, states]] for t in range(terms)], axis=1)
        summed = dot(row, joined[...].reshape(terms * depth, own * depth))
        rows, cols = iota((depth, depth), 0), iota((depth, depth), 1)
        for p in range(own):
            keep = (rows < size) & (cols < width(mine + p))
            result[n, p] = jnp.where(keep, summed[:, p * depth : (p + 1) * depth], 0.0).astype(BF)
        pltpu.make_async_copy(result.at[n], out.at[i], out_sems.at[n]).start()

    for n in range(count):
        pltpu.make_async_copy(result.at[n], out.at[place(n)], out_sems.at[n]).wait()


def apply_blocks(edges, start, stop, own, total, shifts, sizes, packed, carried, two, left, right, halo):
    blocks, states, depth, _ = two.shape
    terms, bonds = packed.shape[0], left.shape[0]
    count = 2 if edges else stop - start
    slots = 6 if edges else count + 2
    smem = pl.BlockSpec(memory_space=pltpu.SMEM)
    vmem = pl.BlockSpec(memory_space=pltpu.VMEM)
    anyw = pl.BlockSpec(memory_space=pl.ANY)
    out_shape = jax.ShapeDtypeStruct((blocks, own, depth, depth), BF)
    spread_shape = jax.ShapeDtypeStruct((terms * own * ROWS, states * ROWS), BF)
    operands = [shifts, sizes, packed]
    in_specs = [smem, smem, vmem]
    if carried is None:
        out_shapes, out_specs, aliases = (out_shape, spread_shape), (anyw, vmem), {}
    else:
        operands += [carried[1], carried[0]]
        in_specs += [vmem, anyw]
        out_shapes, out_specs, aliases = out_shape, anyw, {4: 0}
    operands += [two, left, right, *halo]
    in_specs += [anyw] * (3 + len(halo))
    flops = 2 * count * terms * own * depth**2 * (2 * depth + states * ROWS)
    moved = 2 * depth**2 * (count * (states + bonds + own) + slots * bonds)
    result = pl.pallas_call(
        functools.partial(block_kernel, edges, start, stop, own, total),
        out_shape=out_shapes,
        in_specs=in_specs,
        out_specs=out_specs,
        input_output_aliases=aliases,
        scratch_shapes=[
            pltpu.VMEM((count, states, depth, depth), BF),
            pltpu.VMEM((count, bonds, depth, depth), BF),
            pltpu.VMEM((slots, bonds, depth, depth), BF),
            pltpu.VMEM((terms, own, depth, depth), BF),
            pltpu.VMEM((terms, depth, own * depth), BF),
            pltpu.VMEM((count, own, depth, depth), BF),
            pltpu.VMEM((terms, 128), I32),
            pltpu.SMEM((terms, 128), I32),
            pltpu.SemaphoreType.DMA((3, slots + 2)),
            pltpu.SemaphoreType.DMA((count + 1,)),
        ],
        compiler_params=pltpu.CompilerParams(vmem_limit_bytes=VMEM_LIMIT),
        cost_estimate=pl.CostEstimate(flops=flops, bytes_accessed=moved, transcendentals=0),
        name="edge_blocks" if edges else "inner_blocks",
    )(*operands)
    return result if carried is None else (result, carried[1])


def body(two_site, left_env, right_env, mpo_terms, term_left, term_right, shifts, block_sizes):
    blocks, states = two_site.shape[:2]
    bonds = right_env.shape[0]
    groups, count = lax.axis_size("mpo"), lax.axis_size("blk")
    own, total = states // groups, blocks * count
    half = bonds // 2
    core = lax.rem(lax.axis_index("mpo"), 2)

    up = [(b, b + 1) for b in range(count - 1)]
    down = [(b + 1, b) for b in range(count - 1)]
    swap = [(m, m ^ 1) for m in range(groups)]
    edge = (half, 1, *right_env.shape[2:])
    tail = lax.dynamic_slice(right_env, (core * half, blocks - 1, 0, 0), edge).reshape(half, *edge[2:])
    head = lax.dynamic_slice(right_env, (core * half, 0, 0, 0), edge).reshape(half, *edge[2:])
    below = lax.ppermute(tail, "blk", up)
    above = lax.ppermute(head, "blk", down)

    packed = gathered(pack(term_left, term_right, mpo_terms), "mpo")
    packed = packed.reshape(-1, *packed.shape[2:])
    arrays = (two_site, left_env, right_env)
    sides = (own, total, shifts, block_sizes, packed)
    done = apply_blocks(False, 1, blocks - 1, *sides, None, *arrays, ())
    below, above, done = lax.optimization_barrier((below, above, done))
    below_too = lax.ppermute(below, "mpo", swap)
    above_too = lax.ppermute(above, "mpo", swap)
    done = apply_blocks(True, 0, 0, *sides, done, *arrays, (below, below_too, above, above_too))
    return done[0]


def solution(mesh):
    return jax.shard_map(
        body,
        mesh=mesh,
        in_specs=(
            P("blk", None, None, None),
            P(None, "blk", None, None),
            P(None, "blk", None, None),
            P("mpo", None, None),
            P("mpo"),
            P("mpo"),
            P(),
            P(),
        ),
        out_specs=P("blk", "mpo", None, None),
        check_vma=False,
    )
```

```python
import functools
import math

import jax
import jax.numpy as jnp
from jax import lax
from jax.experimental import pallas as pl
from jax.experimental.pallas import tpu as pltpu
from jax.sharding import PartitionSpec as P

BF, F32, I32 = jnp.bfloat16, jnp.float32, jnp.int32
ROWS = 16
LANES = 128
SPARE_VMEM = 12 * 2**20
MOST_VMEM = 60 * 2**20


def dot(a, b):
    return jnp.dot(a, b, preferred_element_type=F32)


def iota(shape, axis):
    return lax.broadcasted_iota(I32, shape, axis)


def gathered(mine, axis):
    count = lax.axis_size(axis)
    turns = [[(m, (m + turn) % count) for m in range(count)] for turn in range(1, count)]
    return [mine, *(lax.ppermute(mine, axis, pairs) for pairs in turns)]


def ready_kernel(left_ref, right_ref, terms_ref, env_ref, packed_ref, sent_ref, sem):
    terms, states, _ = terms_ref.shape
    core = lax.rem(lax.axis_index("mpo"), 2)
    edge = (1 - core) * (env_ref.shape[1] - 1)
    copy = pltpu.make_async_copy(env_ref.at[:, edge], sent_ref, sem)
    copy.start()
    packed_ref[...] = jnp.zeros_like(packed_ref)
    packed_ref[:, :, :states] = terms_ref[...]
    lane = iota((states, LANES), 1)
    for t in range(terms):
        row = packed_ref[t].astype(F32)
        row = jnp.where(lane == states, left_ref[t].astype(F32), row)
        row = jnp.where(lane == states + 1, right_ref[t].astype(F32), row)
        packed_ref[t] = row.astype(BF)
    copy.wait()


def ready(term_left, term_right, mpo_terms, right_env):
    terms, states, _ = mpo_terms.shape
    bonds, _, depth, _ = right_env.shape
    smem = pl.BlockSpec(memory_space=pltpu.SMEM)
    vmem = pl.BlockSpec(memory_space=pltpu.VMEM)
    anyw = pl.BlockSpec(memory_space=pl.ANY)
    return pl.pallas_call(
        ready_kernel,
        out_shape=[
            pltpu.VMEM((terms, states, LANES), BF),
            pltpu.VMEM((bonds, depth, depth), BF),
        ],
        in_specs=[smem, smem, vmem, anyw],
        out_specs=[vmem, vmem],
        scratch_shapes=[pltpu.SemaphoreType.DMA],
        name="ready",
    )(term_left, term_right, mpo_terms, right_env)


def spread_terms(packed, spread, own, mine):
    terms, states, _ = packed.shape
    width, rows = states * ROWS, own * ROWS
    pick = jnp.where(iota((rows, states), 1) == mine + iota((rows, states), 0) // ROWS, 1.0, 0.0).astype(BF)
    widen = jnp.where(iota((LANES, width), 0) == iota((LANES, width), 1) // ROWS, 1.0, 0.0).astype(BF)
    diagonal = jnp.where(iota((ROWS, width), 0) == iota((ROWS, width), 1) % ROWS, 1.0, 0.0).astype(BF)
    wide = dot(packed[...].reshape(terms * states, LANES), widen).astype(BF)
    for t in range(terms):
        chosen = dot(pick, wide[t * states : (t + 1) * states, :]).astype(BF)
        chosen = chosen.reshape(own, ROWS, width) * diagonal[None]
        spread[t * rows : (t + 1) * rows, :] = chosen.reshape(rows, width)


def block_kernel(edge, count, own, total, *refs):
    refs = list(refs)
    pieces = [refs.pop(0) for _ in range(lax.axis_size("mpo"))]
    numbers = [refs.pop(0) for _ in range(2)]
    if edge:
        refs.pop(0)
        halo = refs.pop(0)
    two, left, right, out = (refs.pop(0) for _ in range(4))
    if edge:
        passed = refs.pop(0)
    packed, spread, clean, lefts, rights, mixed, joined, result, wide, index, shifts, sizes, sems = refs

    blocks, states, depth, _ = two.shape
    terms = packed.shape[0]
    share = terms // len(pieces)
    me = lax.axis_index("mpo")
    core = lax.rem(me, 2)
    first = lax.axis_index("blk") * blocks
    mine = (me - core) * (own // 2) if edge else me * own

    def place(n):
        return core * (blocks - 1) if edge else 1 + n

    def two_copy(n):
        return pltpu.make_async_copy(two.at[place(n)], clean.at[n], sems.at[0, n])

    def left_copy(n):
        return pltpu.make_async_copy(left.at[:, place(n)], lefts.at[n], sems.at[1, n])

    def right_copy(slot):
        if not edge:
            return pltpu.make_async_copy(right.at[:, slot], rights.at[slot], sems.at[2, slot])
        if slot == 0:
            return pltpu.make_async_copy(halo, rights.at[2 * core], sems.at[2, slot])
        near = place(0) + (0 if slot == 1 else 1 - 2 * core)
        return pltpu.make_async_copy(right.at[:, near], rights.at[1 if slot == 1 else 2 - 2 * core], sems.at[2, slot])

    def index_copy():
        return pltpu.make_async_copy(wide, index, sems.at[3, 0])

    small = [
        pltpu.make_async_copy(piece, packed.at[pl.ds(n * share, share)], sems.at[5, n])
        for n, piece in enumerate(pieces)
    ] + [pltpu.make_async_copy(a, b, sems.at[6, n]) for n, (a, b) in enumerate(zip(numbers, (shifts, sizes)))]
    for copy in small:
        copy.start()
    two_copy(0).start()

    def live(n, p=None):
        j = first + place(n) + (0 if p is None else shifts[p])
        return jnp.where((j >= 0) & (j < total), sizes[jnp.clip(j, 0, total - 1)], 0)

    def wipe(n):
        keep_rows = jnp.where(iota((depth, depth), 0) < live(n), 1.0, 0.0).astype(BF)
        lane = iota((ROWS, depth), 1)
        for q in range(states):
            keep_cols = jnp.where(lane < live(n, q), 1.0, 0.0).astype(BF)
            block = clean[n, q].reshape(depth // ROWS, ROWS, depth) * keep_cols[None]
            clean[n, q] = block.reshape(depth, depth) * keep_rows

    for copy in small:
        copy.wait()
    wide[...] = packed[:, 0, :].astype(F32).astype(I32)
    index_copy().start()
    spread_terms(packed, spread, own, mine)
    two_copy(0).wait()
    wipe(0)
    for n in range(count):
        for slot in (0, 1, 2) if n == 0 else (n + 2,):
            right_copy(slot).start()
        left_copy(n).start()
        if n + 1 < count:
            two_copy(n + 1).start()
    index_copy().wait()

    def apply(n):
        i = place(n)

        for h in range(depth // (2 * ROWS)):
            spans = [slice((2 * h + u) * ROWS, (2 * h + u + 1) * ROWS) for u in range(2)]
            both = jnp.concatenate(
                [clean[n, :, s, :].reshape(states * ROWS, depth) for s in spans], axis=1
            )
            part = dot(spread[...], both).astype(BF).reshape(terms, own, ROWS, 2 * depth)
            for u in range(2):
                mixed[:, :, spans[u], :] = part[:, :, :, u * depth : (u + 1) * depth]

        if edge:
            for slot in range(3):
                right_copy(slot).wait()
        else:

            @pl.when(n == 0)
            def _():
                right_copy(0).wait()
                right_copy(1).wait()

            right_copy(n + 2).wait()
        if not edge:
            later = jnp.minimum(n + 1, count - 1)

            @pl.when(n + 1 < count)
            def _():
                two_copy(n + 1).wait()

            wipe(later)
        slot_of = [(1 if edge else n + 1) + shifts[mine + p] for p in range(own)]
        for t in range(terms):
            bond = index[t, states + 1]
            for p in range(own):
                joined[t, :, p * depth : (p + 1) * depth] = dot(
                    mixed[t, p], rights[slot_of[p], bond]
                ).astype(BF)

        left_copy(n).wait()
        row = jnp.concatenate([lefts[n, index[t, states]] for t in range(terms)], axis=1)
        summed = dot(row, joined[...].reshape(terms * depth, own * depth))
        rows, cols = iota((depth, depth), 0), iota((depth, depth), 1)
        for p in range(own):
            keep = (rows < live(n)) & (cols < live(n, mine + p))
            result[n, p] = jnp.where(keep, summed[:, p * depth : (p + 1) * depth], 0.0).astype(BF)

    if edge:
        apply(0)
        half = own // 2
        ours = pltpu.make_async_copy(
            result.at[0, pl.ds(core * half, half)], out.at[place(0)], sems.at[0, 0]
        )
        theirs = pltpu.make_async_copy(
            result.at[0, pl.ds((1 - core) * half, half)], passed, sems.at[1, 0]
        )
        theirs.start()
        ours.start()
        theirs.wait()
        ours.wait()
    else:

        def out_copy(n):
            return pltpu.make_async_copy(result.at[n], out.at[place(n)], sems.at[4, n])

        @pl.loop(0, count)
        def _(n):
            apply(n)
            out_copy(n).start()

        for n in range(count):
            out_copy(n).wait()


def apply_blocks(edge, pieces, shifts, sizes, two, left, right, own, total, done=None, halo=None):
    blocks, states, depth, _ = two.shape
    terms, bonds = sum(piece.shape[0] for piece in pieces), left.shape[0]
    count = 1 if edge else blocks - 2
    slots = count + 2
    anyw = pl.BlockSpec(memory_space=pl.ANY)
    near = functools.partial(pltpu.with_memory_space_constraint, memory_space=pltpu.VMEM)
    far = functools.partial(pltpu.with_memory_space_constraint, memory_space=pltpu.HBM)
    operands = [*map(near, pieces), far(shifts), far(sizes)]
    operands += [far(done), near(halo)] if edge else []
    operands += map(far, (two, left, right))
    kept = own // 2 if edge else own
    out_shapes = [jax.ShapeDtypeStruct((blocks, kept, depth, depth), BF)]
    if edge:
        out_shapes.append(jax.ShapeDtypeStruct((kept, depth, depth), BF))
    buffers = [
        (terms, states, LANES),
        (terms * own * ROWS, states * ROWS),
        (count, states, depth, depth),
        (count, bonds, depth, depth),
        (slots, bonds, depth, depth),
        (terms, own, depth, depth),
        (terms, depth, own * depth),
        (count, own, depth, depth),
    ]
    held = sum(2 * math.prod(shape) for shape in buffers)
    flops = 2 * count * terms * own * depth**2 * (2 * depth + states * ROWS)
    moved = 2 * depth**2 * (count * (states + bonds + own) + slots * bonds)
    return pl.pallas_call(
        functools.partial(block_kernel, edge, count, own, total),
        out_shape=out_shapes,
        in_specs=[anyw] * len(operands),
        out_specs=[anyw] * len(out_shapes),
        input_output_aliases={len(pieces) + 2: 0} if edge else {},
        scratch_shapes=[
            *(pltpu.VMEM(shape, BF) for shape in buffers),
            pltpu.VMEM((terms, LANES), I32),
            pltpu.SMEM((terms, LANES), I32),
            pltpu.SMEM(shifts.shape, I32),
            pltpu.SMEM(sizes.shape, I32),
            pltpu.SemaphoreType.DMA((7, max(slots, len(pieces)))),
        ],
        compiler_params=pltpu.CompilerParams(vmem_limit_bytes=min(held + SPARE_VMEM, MOST_VMEM)),
        cost_estimate=pl.CostEstimate(flops=flops, bytes_accessed=moved, transcendentals=0),
        name="edge_block" if edge else "inner_blocks",
    )(*operands)


def body(two_site, left_env, right_env, mpo_terms, term_left, term_right, shifts, block_sizes):
    blocks, states = two_site.shape[:2]
    groups, count = lax.axis_size("mpo"), lax.axis_size("blk")
    own, total = states // groups, blocks * count
    core = lax.rem(lax.axis_index("mpo"), 2)

    packed, sent = ready(term_left, term_right, mpo_terms, right_env)
    pieces = gathered(packed, "mpo")

    place = lambda m, b: m * count + b
    up = [(place(m, b), place(m, b + 1)) for m in range(0, groups, 2) for b in range(count - 1)]
    down = [(place(m, b + 1), place(m, b)) for m in range(1, groups, 2) for b in range(count - 1)]
    halo = lax.ppermute(sent, ("mpo", "blk"), up + down)

    arrays = (pieces, shifts, block_sizes, two_site, left_env, right_env)
    (done,) = apply_blocks(False, *arrays, own, total)
    done, passed = apply_blocks(True, *arrays, 2 * own, total, done, halo)
    passed = lax.ppermute(passed, "mpo", [(m, m ^ 1) for m in range(groups)])
    return lax.dynamic_update_slice(done, passed[None], ((1 - core) * (blocks - 1), 0, 0, 0))


def solution(mesh):
    return jax.shard_map(
        body,
        mesh=mesh,
        in_specs=(
            P("blk", None, None, None),
            P(None, "blk", None, None),
            P(None, "blk", None, None),
            P("mpo", None, None),
            P("mpo"),
            P("mpo"),
            P(),
            P(),
        ),
        out_specs=P("blk", "mpo", None, None),
        check_vma=False,
    )
```

```python
import functools
import math

import jax
import jax.numpy as jnp
from jax import lax
from jax.experimental import pallas as pl
from jax.experimental.pallas import tpu as pltpu
from jax.sharding import PartitionSpec as P

BF, F32, I32 = jnp.bfloat16, jnp.float32, jnp.int32
ROWS = 16
LANES = 128
CUTS = 4
SPARE_VMEM = 12 * 2**20
MOST_VMEM = 60 * 2**20


def dot(a, b):
    return jnp.dot(a, b, preferred_element_type=F32)


def iota(shape, axis):
    return lax.broadcasted_iota(I32, shape, axis)


def gathered(mine, axis):
    count = lax.axis_size(axis)
    turns = [[(m, (m + turn) % count) for m in range(count)] for turn in range(1, count)]
    return [mine, *(lax.ppermute(mine, axis, pairs) for pairs in turns)]


def ready_kernel(left_ref, right_ref, terms_ref, env_ref, packed_ref, sent_ref, sems):
    terms, states, _ = terms_ref.shape
    core = lax.rem(lax.axis_index("mpo"), 2)
    edge = (1 - core) * (env_ref.shape[1] - 1)
    share = -(-sent_ref.shape[0] // CUTS)
    copies = []
    for cut in range(CUTS):
        span = pl.ds(cut * share, min(share, sent_ref.shape[0] - cut * share))
        copies.append(pltpu.make_async_copy(env_ref.at[span, edge], sent_ref.at[span], sems.at[cut]))
        copies[-1].start()
    packed_ref[...] = jnp.zeros_like(packed_ref)
    packed_ref[:, :, :states] = terms_ref[...]
    lane = iota((states, LANES), 1)
    for t in range(terms):
        row = packed_ref[t].astype(F32)
        row = jnp.where(lane == states, left_ref[t].astype(F32), row)
        row = jnp.where(lane == states + 1, right_ref[t].astype(F32), row)
        packed_ref[t] = row.astype(BF)
    for copy in copies:
        copy.wait()


def ready(term_left, term_right, mpo_terms, right_env):
    terms, states, _ = mpo_terms.shape
    bonds, _, depth, _ = right_env.shape
    smem = pl.BlockSpec(memory_space=pltpu.SMEM)
    vmem = pl.BlockSpec(memory_space=pltpu.VMEM)
    anyw = pl.BlockSpec(memory_space=pl.ANY)
    return pl.pallas_call(
        ready_kernel,
        out_shape=[
            pltpu.VMEM((terms, states, LANES), BF),
            pltpu.VMEM((bonds, depth, depth), BF),
        ],
        in_specs=[smem, smem, vmem, anyw],
        out_specs=[vmem, vmem],
        scratch_shapes=[pltpu.SemaphoreType.DMA((CUTS,))],
        name="ready",
    )(term_left, term_right, mpo_terms, right_env)


def spread_terms(packed, spread, own, mine):
    terms, states, _ = packed.shape
    width, rows = states * ROWS, own * ROWS
    pick = jnp.where(iota((rows, states), 1) == mine + iota((rows, states), 0) // ROWS, 1.0, 0.0).astype(BF)
    widen = jnp.where(iota((LANES, width), 0) == iota((LANES, width), 1) // ROWS, 1.0, 0.0).astype(BF)
    diagonal = jnp.where(iota((ROWS, width), 0) == iota((ROWS, width), 1) % ROWS, 1.0, 0.0).astype(BF)
    wide = dot(packed[...].reshape(terms * states, LANES), widen).astype(BF)
    for t in range(terms):
        chosen = dot(pick, wide[t * states : (t + 1) * states, :]).astype(BF)
        chosen = chosen.reshape(own, ROWS, width) * diagonal[None]
        spread[t * rows : (t + 1) * rows, :] = chosen.reshape(rows, width)


def block_kernel(edge, count, own, total, *refs):
    refs = list(refs)
    pieces = [refs.pop(0) for _ in range(lax.axis_size("mpo"))]
    numbers = [refs.pop(0) for _ in range(2)]
    if edge:
        refs.pop(0)
        halo = refs.pop(0)
    two, left, right, out = (refs.pop(0) for _ in range(4))
    if edge:
        passed = refs.pop(0)
    spread, keeps, clean, lefts, rights, mixed, joined, result, wide, index, shifts, sizes, sems = refs

    blocks, states, depth, _ = two.shape
    share = pieces[0].shape[0]
    terms = share * len(pieces)
    me = lax.axis_index("mpo")
    core = lax.rem(me, 2)
    first = lax.axis_index("blk") * blocks
    mine = (me - core) * (own // 2) if edge else me * own

    def place(n):
        return core * (blocks - 1) if edge else 1 + n

    def two_copy(n):
        return pltpu.make_async_copy(two.at[place(n)], clean.at[n], sems.at[0, n])

    def left_copy(n):
        return pltpu.make_async_copy(left.at[:, place(n)], lefts.at[n], sems.at[1, n])

    def right_copy(slot):
        if not edge:
            return pltpu.make_async_copy(right.at[:, slot], rights.at[slot], sems.at[2, slot])
        if slot == 0:
            return pltpu.make_async_copy(halo, rights.at[2 * core], sems.at[2, slot])
        near = place(0) + (0 if slot == 1 else 1 - 2 * core)
        return pltpu.make_async_copy(right.at[:, near], rights.at[1 if slot == 1 else 2 - 2 * core], sems.at[2, slot])

    def index_copy():
        return pltpu.make_async_copy(wide, index, sems.at[3, 0])

    small = [
        pltpu.make_async_copy(a, b, sems.at[5, n]) for n, (a, b) in enumerate(zip(numbers, (shifts, sizes)))
    ]
    for copy in small:
        copy.start()
    two_copy(0).start()
    for slot in range(3):
        right_copy(slot).start()
    left_copy(0).start()
    for n, piece in enumerate(pieces):
        wide[n * share : (n + 1) * share, :] = piece[:, 0, :].astype(F32).astype(I32)
    index_copy().start()
    for n, piece in enumerate(pieces):
        spread_terms(piece, spread.at[pl.ds(n * share * own * ROWS, share * own * ROWS)], own, mine)
    for copy in small:
        copy.wait()

    def live(slot):
        j = first + place(0) - 1 + slot
        return jnp.where((j >= 0) & (j < total), sizes[jnp.clip(j, 0, total - 1)], 0)

    for slot in range(count + 2):
        keeps[slot] = jnp.where(iota((ROWS, depth), 1) < live(slot), 1.0, 0.0).astype(BF)
    two_copy(0).wait()
    for n in range(1, count):
        two_copy(n).start()
        right_copy(n + 2).start()
        left_copy(n).start()

    def apply(n, leading):
        size = live(n + 1)
        if not leading:
            two_copy(n).wait()
            right_copy(n + 2).wait()
            left_copy(n).wait()

        for h in range(depth // (2 * ROWS)):
            spans = [slice((2 * h + u) * ROWS, (2 * h + u + 1) * ROWS) for u in range(2)]
            both = []
            for s in spans:
                keep_rows = jnp.where(iota((ROWS, depth), 0) + s.start < size, 1.0, 0.0).astype(BF)
                both.append([clean[n, q, s, :] * keeps[n + 1 + shifts[q]] * keep_rows for q in range(states)])
            both = jnp.concatenate([jnp.concatenate(tiles, axis=0) for tiles in both], axis=1)
            part = dot(spread[...], both).astype(BF).reshape(terms, own, ROWS, 2 * depth)
            for u in range(2):
                mixed[:, :, spans[u], :] = part[:, :, :, u * depth : (u + 1) * depth]

        if leading:
            index_copy().wait()
            for slot in range(3):
                right_copy(slot).wait()
        slot_of = [n + 1 + shifts[mine + p] for p in range(own)]
        for t in range(terms):
            bond = index[t, states + 1]
            for p in range(own):
                joined[t, :, p * depth : (p + 1) * depth] = dot(
                    mixed[t, p], rights[slot_of[p], bond]
                ).astype(BF)

        if leading:
            left_copy(n).wait()
        row = jnp.concatenate([lefts[n, index[t, states]] for t in range(terms)], axis=1)
        summed = dot(row, joined[...].reshape(terms * depth, own * depth))
        keep_rows = jnp.where(iota((depth, depth), 0) < size, 1.0, 0.0)
        for p in range(own):
            keep = keep_rows * keeps[slot_of[p], :1, :].astype(F32)
            result[n, p] = (summed[:, p * depth : (p + 1) * depth] * keep).astype(BF)

    if edge:
        apply(0, True)
        half = own // 2
        ours = pltpu.make_async_copy(
            result.at[0, pl.ds(core * half, half)], out.at[place(0)], sems.at[0, 0]
        )
        theirs = pltpu.make_async_copy(
            result.at[0, pl.ds((1 - core) * half, half)], passed, sems.at[1, 0]
        )
        theirs.start()
        ours.start()
        theirs.wait()
        ours.wait()
    else:

        def out_copy(n):
            return pltpu.make_async_copy(result.at[n], out.at[place(n)], sems.at[4, n])

        apply(0, True)
        out_copy(0).start()

        @pl.loop(1, count)
        def _(n):
            apply(n, False)
            out_copy(n).start()

        for n in range(count):
            out_copy(n).wait()


def apply_blocks(edge, pieces, shifts, sizes, two, left, right, own, total, done=None, halo=None):
    blocks, states, depth, _ = two.shape
    terms, bonds = sum(piece.shape[0] for piece in pieces), left.shape[0]
    count = 1 if edge else blocks - 2
    slots = count + 2
    anyw = pl.BlockSpec(memory_space=pl.ANY)
    vmem = pl.BlockSpec(memory_space=pltpu.VMEM)
    near = functools.partial(pltpu.with_memory_space_constraint, memory_space=pltpu.VMEM)
    far = functools.partial(pltpu.with_memory_space_constraint, memory_space=pltpu.HBM)
    operands = [*map(near, pieces), far(shifts), far(sizes)]
    operands += [far(done), near(halo)] if edge else []
    operands += map(far, (two, left, right))
    kept = own // 2 if edge else own
    out_shapes = [jax.ShapeDtypeStruct((blocks, kept, depth, depth), BF)]
    if edge:
        out_shapes.append(jax.ShapeDtypeStruct((kept, depth, depth), BF))
    buffers = [
        (terms * own * ROWS, states * ROWS),
        (slots, ROWS, depth),
        (count, states, depth, depth),
        (count, bonds, depth, depth),
        (slots, bonds, depth, depth),
        (terms, own, depth, depth),
        (terms, depth, own * depth),
        (count, own, depth, depth),
    ]
    held = sum(2 * math.prod(shape) for shape in buffers)
    return pl.pallas_call(
        functools.partial(block_kernel, edge, count, own, total),
        out_shape=out_shapes,
        in_specs=[vmem] * len(pieces) + [anyw] * (len(operands) - len(pieces)),
        out_specs=[anyw] * len(out_shapes),
        input_output_aliases={len(pieces) + 2: 0} if edge else {},
        scratch_shapes=[
            *(pltpu.VMEM(shape, BF) for shape in buffers),
            pltpu.VMEM((terms, LANES), I32),
            pltpu.SMEM((terms, LANES), I32),
            pltpu.SMEM(shifts.shape, I32),
            pltpu.SMEM(sizes.shape, I32),
            pltpu.SemaphoreType.DMA((6, slots)),
        ],
        compiler_params=pltpu.CompilerParams(vmem_limit_bytes=min(held + SPARE_VMEM, MOST_VMEM)),
        name="edge_block" if edge else "inner_blocks",
    )(*operands)


def body(two_site, left_env, right_env, mpo_terms, term_left, term_right, shifts, block_sizes):
    blocks, states = two_site.shape[:2]
    groups, count = lax.axis_size("mpo"), lax.axis_size("blk")
    own, total = states // groups, blocks * count
    core = lax.rem(lax.axis_index("mpo"), 2)

    packed, sent = ready(term_left, term_right, mpo_terms, right_env)
    place = lambda m, b: m * count + b
    up = [(place(m, b), place(m, b + 1)) for m in range(0, groups, 2) for b in range(count - 1)]
    down = [(place(m, b + 1), place(m, b)) for m in range(1, groups, 2) for b in range(count - 1)]
    halo = lax.ppermute(sent, ("mpo", "blk"), up + down)
    pieces = gathered(packed, "mpo")

    arrays = (pieces, shifts, block_sizes, two_site, left_env, right_env)
    (done,) = apply_blocks(False, *arrays, own, total)
    done, passed = apply_blocks(True, *arrays, 2 * own, total, done, halo)
    passed = lax.ppermute(passed, "mpo", [(m, m ^ 1) for m in range(groups)])
    return lax.dynamic_update_slice(done, passed[None], ((1 - core) * (blocks - 1), 0, 0, 0))


def solution(mesh):
    return jax.shard_map(
        body,
        mesh=mesh,
        in_specs=(
            P("blk", None, None, None),
            P(None, "blk", None, None),
            P(None, "blk", None, None),
            P("mpo", None, None),
            P("mpo"),
            P("mpo"),
            P(),
            P(),
        ),
        out_specs=P("blk", "mpo", None, None),
        check_vma=False,
    )
```

```python
import functools
import math

import jax
import jax.numpy as jnp
from jax import lax
from jax.experimental import pallas as pl
from jax.experimental.pallas import tpu as pltpu
from jax.sharding import PartitionSpec as P

BF, F32, I32 = jnp.bfloat16, jnp.float32, jnp.int32
ROWS = 16
LANES = 128
CUTS = 4
SPARE_VMEM = 12 * 2**20
MOST_VMEM = 60 * 2**20


def dot(a, b):
    return jnp.dot(a, b, preferred_element_type=F32)


def iota(shape, axis):
    return lax.broadcasted_iota(I32, shape, axis)


def gathered(mine, axis):
    count = lax.axis_size(axis)
    turns = [[(m, (m + turn) % count) for m in range(count)] for turn in range(1, count)]
    return [mine, *(lax.ppermute(mine, axis, pairs) for pairs in turns)]


def ready_kernel(left_hbm, right_hbm, terms_hbm, env_ref, packed_ref, sent_ref, left_ref, right_ref, terms_ref, sems):
    terms, states, _ = terms_ref.shape
    small = [
        pltpu.make_async_copy(a, b, sems.at[CUTS + n])
        for n, (a, b) in enumerate(((left_hbm, left_ref), (right_hbm, right_ref), (terms_hbm, terms_ref)))
    ]
    for copy in small:
        copy.start()
    core = lax.rem(lax.axis_index("mpo"), 2)
    edge = (1 - core) * (env_ref.shape[1] - 1)
    share = -(-sent_ref.shape[0] // CUTS)
    copies = []
    for cut in range(CUTS):
        span = pl.ds(cut * share, min(share, sent_ref.shape[0] - cut * share))
        copies.append(pltpu.make_async_copy(env_ref.at[span, edge], sent_ref.at[span], sems.at[cut]))
        copies[-1].start()
    for copy in small:
        copy.wait()
    packed_ref[...] = jnp.zeros_like(packed_ref)
    packed_ref[:, :, :states] = terms_ref[...]
    lane = iota((states, LANES), 1)
    for t in range(terms):
        row = packed_ref[t].astype(F32)
        row = jnp.where(lane == states, left_ref[t].astype(F32), row)
        row = jnp.where(lane == states + 1, right_ref[t].astype(F32), row)
        packed_ref[t] = row.astype(BF)
    for copy in copies:
        copy.wait()


def ready(term_left, term_right, mpo_terms, right_env):
    terms, states, _ = mpo_terms.shape
    bonds, _, depth, _ = right_env.shape
    vmem = pl.BlockSpec(memory_space=pltpu.VMEM)
    anyw = pl.BlockSpec(memory_space=pl.ANY)
    return pl.pallas_call(
        ready_kernel,
        out_shape=[
            pltpu.VMEM((terms, states, LANES), BF),
            pltpu.VMEM((bonds, depth, depth), BF),
        ],
        in_specs=[anyw] * 4,
        out_specs=[vmem, vmem],
        scratch_shapes=[
            pltpu.SMEM((terms,), I32),
            pltpu.SMEM((terms,), I32),
            pltpu.VMEM(mpo_terms.shape, BF),
            pltpu.SemaphoreType.DMA((CUTS + 3,)),
        ],
        name="ready",
    )(*(pltpu.with_memory_space_constraint(x, pltpu.HBM) for x in (term_left, term_right, mpo_terms, right_env)))


def spread_terms(packed, spread, own, mine):
    terms, states, _ = packed.shape
    width, rows = states * ROWS, own * ROWS
    pick = jnp.where(iota((rows, states), 1) == mine + iota((rows, states), 0) // ROWS, 1.0, 0.0).astype(BF)
    widen = jnp.where(iota((LANES, width), 0) == iota((LANES, width), 1) // ROWS, 1.0, 0.0).astype(BF)
    diagonal = jnp.where(iota((ROWS, width), 0) == iota((ROWS, width), 1) % ROWS, 1.0, 0.0).astype(BF)
    wide = dot(packed[...].reshape(terms * states, LANES), widen).astype(BF)
    for t in range(terms):
        chosen = dot(pick, wide[t * states : (t + 1) * states, :]).astype(BF)
        chosen = chosen.reshape(own, ROWS, width) * diagonal[None]
        spread[t * rows : (t + 1) * rows, :] = chosen.reshape(rows, width)


def block_kernel(edge, count, own, total, *refs):
    refs = list(refs)
    pieces = [refs.pop(0) for _ in range(lax.axis_size("mpo"))]
    numbers = [refs.pop(0) for _ in range(2)]
    if edge:
        refs.pop(0)
        halo = refs.pop(0)
    two, left, right, out = (refs.pop(0) for _ in range(4))
    if edge:
        passed = refs.pop(0)
    spread, keeps, clean, lefts, rights, mixed, joined, result, wide, index, shifts, sizes, sems = refs

    blocks, states, depth, _ = two.shape
    share = pieces[0].shape[0]
    terms = share * len(pieces)
    me = lax.axis_index("mpo")
    core = lax.rem(me, 2)
    first = lax.axis_index("blk") * blocks
    mine = (me - core) * (own // 2) if edge else me * own

    def place(n):
        return core * (blocks - 1) if edge else 1 + n

    def two_copy(n):
        return pltpu.make_async_copy(two.at[place(n)], clean.at[n], sems.at[0, n])

    def left_copy(n):
        return pltpu.make_async_copy(left.at[:, place(n)], lefts.at[n], sems.at[1, n])

    def right_copy(slot):
        if not edge:
            return pltpu.make_async_copy(right.at[:, slot], rights.at[slot], sems.at[2, slot])
        if slot == 0:
            return pltpu.make_async_copy(halo, rights.at[2 * core], sems.at[2, slot])
        near = place(0) + (0 if slot == 1 else 1 - 2 * core)
        return pltpu.make_async_copy(right.at[:, near], rights.at[1 if slot == 1 else 2 - 2 * core], sems.at[2, slot])

    def index_copy():
        return pltpu.make_async_copy(wide, index, sems.at[3, 0])

    small = [
        pltpu.make_async_copy(a, b, sems.at[5, n]) for n, (a, b) in enumerate(zip(numbers, (shifts, sizes)))
    ]
    for copy in small:
        copy.start()
    two_copy(0).start()
    for slot in range(3):
        right_copy(slot).start()
    left_copy(0).start()
    for n, piece in enumerate(pieces):
        wide[n * share : (n + 1) * share, :] = piece[:, 0, :].astype(F32).astype(I32)
    index_copy().start()
    for n, piece in enumerate(pieces):
        spread_terms(piece, spread.at[pl.ds(n * share * own * ROWS, share * own * ROWS)], own, mine)
    for copy in small:
        copy.wait()

    def live(slot):
        j = first + place(0) - 1 + slot
        return jnp.where((j >= 0) & (j < total), sizes[jnp.clip(j, 0, total - 1)], 0)

    for slot in range(count + 2):
        keeps[slot] = jnp.where(iota((ROWS, depth), 1) < live(slot), 1.0, 0.0).astype(BF)
    two_copy(0).wait()
    for n in range(1, count):
        two_copy(n).start()
        right_copy(n + 2).start()
        left_copy(n).start()

    def apply(n, leading):
        size = live(n + 1)
        if not leading:
            two_copy(n).wait()
            right_copy(n + 2).wait()
            left_copy(n).wait()

        for h in range(depth // (2 * ROWS)):
            spans = [slice((2 * h + u) * ROWS, (2 * h + u + 1) * ROWS) for u in range(2)]
            both = []
            for s in spans:
                keep_rows = jnp.where(iota((ROWS, depth), 0) + s.start < size, 1.0, 0.0).astype(BF)
                both.append([clean[n, q, s, :] * keeps[n + 1 + shifts[q]] * keep_rows for q in range(states)])
            both = jnp.concatenate([jnp.concatenate(tiles, axis=0) for tiles in both], axis=1)
            part = dot(spread[...], both).astype(BF).reshape(terms, own, ROWS, 2 * depth)
            for u in range(2):
                mixed[:, :, spans[u], :] = part[:, :, :, u * depth : (u + 1) * depth]

        if leading:
            index_copy().wait()
            for slot in range(3):
                right_copy(slot).wait()
        slot_of = [n + 1 + shifts[mine + p] for p in range(own)]
        for t in range(terms):
            bond = index[t, states + 1]
            for p in range(own):
                joined[t, :, p * depth : (p + 1) * depth] = dot(
                    mixed[t, p], rights[slot_of[p], bond]
                ).astype(BF)

        if leading:
            left_copy(n).wait()
        row = jnp.concatenate([lefts[n, index[t, states]] for t in range(terms)], axis=1)
        summed = dot(row, joined[...].reshape(terms * depth, own * depth))
        keep_rows = jnp.where(iota((depth, depth), 0) < size, 1.0, 0.0)
        for p in range(own):
            keep = keep_rows * keeps[slot_of[p], :1, :].astype(F32)
            result[n, p] = (summed[:, p * depth : (p + 1) * depth] * keep).astype(BF)

    if edge:
        apply(0, True)
        half = own // 2
        ours = pltpu.make_async_copy(
            result.at[0, pl.ds(core * half, half)], out.at[place(0)], sems.at[0, 0]
        )
        theirs = pltpu.make_async_copy(
            result.at[0, pl.ds((1 - core) * half, half)], passed, sems.at[1, 0]
        )
        theirs.start()
        ours.start()
        theirs.wait()
        ours.wait()
    else:

        def out_copy(n):
            return pltpu.make_async_copy(result.at[n], out.at[place(n)], sems.at[4, n])

        apply(0, True)
        out_copy(0).start()

        @pl.loop(1, count)
        def _(n):
            apply(n, False)
            out_copy(n).start()

        for n in range(count):
            out_copy(n).wait()


def apply_blocks(edge, pieces, shifts, sizes, two, left, right, own, total, done=None, halo=None):
    blocks, states, depth, _ = two.shape
    terms, bonds = sum(piece.shape[0] for piece in pieces), left.shape[0]
    count = 1 if edge else blocks - 2
    slots = count + 2
    anyw = pl.BlockSpec(memory_space=pl.ANY)
    vmem = pl.BlockSpec(memory_space=pltpu.VMEM)
    near = functools.partial(pltpu.with_memory_space_constraint, memory_space=pltpu.VMEM)
    far = functools.partial(pltpu.with_memory_space_constraint, memory_space=pltpu.HBM)
    operands = [*map(near, pieces), far(shifts), far(sizes)]
    operands += [far(done), near(halo)] if edge else []
    operands += map(far, (two, left, right))
    kept = own // 2 if edge else own
    out_shapes = [jax.ShapeDtypeStruct((blocks, kept, depth, depth), BF)]
    if edge:
        out_shapes.append(jax.ShapeDtypeStruct((kept, depth, depth), BF))
    buffers = [
        (terms * own * ROWS, states * ROWS),
        (slots, ROWS, depth),
        (count, states, depth, depth),
        (count, bonds, depth, depth),
        (slots, bonds, depth, depth),
        (terms, own, depth, depth),
        (terms, depth, own * depth),
        (count, own, depth, depth),
    ]
    held = sum(2 * math.prod(shape) for shape in buffers)
    return pl.pallas_call(
        functools.partial(block_kernel, edge, count, own, total),
        out_shape=out_shapes,
        in_specs=[vmem] * len(pieces) + [anyw] * (len(operands) - len(pieces)),
        out_specs=[anyw] * len(out_shapes),
        input_output_aliases={len(pieces) + 2: 0} if edge else {},
        scratch_shapes=[
            *(pltpu.VMEM(shape, BF) for shape in buffers),
            pltpu.VMEM((terms, LANES), I32),
            pltpu.SMEM((terms, LANES), I32),
            pltpu.SMEM(shifts.shape, I32),
            pltpu.SMEM(sizes.shape, I32),
            pltpu.SemaphoreType.DMA((6, slots)),
        ],
        compiler_params=pltpu.CompilerParams(vmem_limit_bytes=min(held + SPARE_VMEM, MOST_VMEM)),
        name="edge_block" if edge else "inner_blocks",
    )(*operands)


def body(two_site, left_env, right_env, mpo_terms, term_left, term_right, shifts, block_sizes):
    blocks, states = two_site.shape[:2]
    groups, count = lax.axis_size("mpo"), lax.axis_size("blk")
    own, total = states // groups, blocks * count
    core = lax.rem(lax.axis_index("mpo"), 2)

    packed, sent = ready(term_left, term_right, mpo_terms, right_env)
    place = lambda m, b: m * count + b
    up = [(place(m, b), place(m, b + 1)) for m in range(0, groups, 2) for b in range(count - 1)]
    down = [(place(m, b + 1), place(m, b)) for m in range(1, groups, 2) for b in range(count - 1)]
    halo = lax.ppermute(sent, ("mpo", "blk"), up + down)
    pieces = gathered(packed, "mpo")

    arrays = (pieces, shifts, block_sizes, two_site, left_env, right_env)
    (done,) = apply_blocks(False, *arrays, own, total)
    done, passed = apply_blocks(True, *arrays, 2 * own, total, done, halo)
    passed = lax.ppermute(passed, "mpo", [(m, m ^ 1) for m in range(groups)])
    return lax.dynamic_update_slice(done, passed[None], ((1 - core) * (blocks - 1), 0, 0, 0))


def solution(mesh):
    return jax.shard_map(
        body,
        mesh=mesh,
        in_specs=(
            P("blk", None, None, None),
            P(None, "blk", None, None),
            P(None, "blk", None, None),
            P("mpo", None, None),
            P("mpo"),
            P("mpo"),
            P(),
            P(),
        ),
        out_specs=P("blk", "mpo", None, None),
        check_vma=False,
    )
```

```python
import functools
import math

import jax
import jax.numpy as jnp
from jax import lax
from jax.experimental import pallas as pl
from jax.experimental.pallas import tpu as pltpu
from jax.sharding import PartitionSpec as P

BF, F32, I32 = jnp.bfloat16, jnp.float32, jnp.int32
ROWS = 16
LANES = 128
CUTS = 4
SPARE_VMEM = 12 * 2**20
MOST_VMEM = 60 * 2**20


def dot(a, b):
    return jnp.dot(a, b, preferred_element_type=F32)


def iota(shape, axis):
    return lax.broadcasted_iota(I32, shape, axis)


def gathered(mine, axis):
    count = lax.axis_size(axis)
    paired = count & (count - 1) == 0
    turns = [
        [(m, m ^ turn if paired else (m + turn) % count) for m in range(count)] for turn in range(1, count)
    ]
    return [mine, *(lax.ppermute(mine, axis, pairs) for pairs in turns)]


def ready_kernel(left_hbm, right_hbm, terms_hbm, env_ref, packed_ref, sent_ref, left_ref, right_ref, terms_ref, sems):
    terms, states, _ = terms_ref.shape
    small = [
        pltpu.make_async_copy(a, b, sems.at[CUTS + n])
        for n, (a, b) in enumerate(((left_hbm, left_ref), (right_hbm, right_ref), (terms_hbm, terms_ref)))
    ]
    for copy in small:
        copy.start()
    core = lax.rem(lax.axis_index("mpo"), 2)
    edge = (1 - core) * (env_ref.shape[1] - 1)
    share = -(-sent_ref.shape[0] // CUTS)
    copies = []
    for cut in range(CUTS):
        span = pl.ds(cut * share, min(share, sent_ref.shape[0] - cut * share))
        copies.append(pltpu.make_async_copy(env_ref.at[span, edge], sent_ref.at[span], sems.at[cut]))
        copies[-1].start()
    for copy in small:
        copy.wait()
    packed_ref[...] = jnp.zeros_like(packed_ref)
    packed_ref[:, :, :states] = terms_ref[...]
    lane = iota((states, LANES), 1)
    for t in range(terms):
        row = packed_ref[t].astype(F32)
        row = jnp.where(lane == states, left_ref[t].astype(F32), row)
        row = jnp.where(lane == states + 1, right_ref[t].astype(F32), row)
        packed_ref[t] = row.astype(BF)
    for copy in copies:
        copy.wait()


def ready(term_left, term_right, mpo_terms, right_env):
    terms, states, _ = mpo_terms.shape
    bonds, _, depth, _ = right_env.shape
    vmem = pl.BlockSpec(memory_space=pltpu.VMEM)
    anyw = pl.BlockSpec(memory_space=pl.ANY)
    return pl.pallas_call(
        ready_kernel,
        out_shape=[
            pltpu.VMEM((terms, states, LANES), BF),
            pltpu.VMEM((bonds, depth, depth), BF),
        ],
        in_specs=[anyw] * 4,
        out_specs=[vmem, vmem],
        scratch_shapes=[
            pltpu.SMEM((terms,), I32),
            pltpu.SMEM((terms,), I32),
            pltpu.VMEM(mpo_terms.shape, BF),
            pltpu.SemaphoreType.DMA((CUTS + 3,)),
        ],
        name="ready",
    )(*(pltpu.with_memory_space_constraint(x, pltpu.HBM) for x in (term_left, term_right, mpo_terms, right_env)))


def spread_terms(packed, spread, own, mine):
    terms, states, _ = packed.shape
    width, rows = states * ROWS, own * ROWS
    pick = jnp.where(iota((rows, states), 1) == mine + iota((rows, states), 0) // ROWS, 1.0, 0.0).astype(BF)
    widen = jnp.where(iota((LANES, width), 0) == iota((LANES, width), 1) // ROWS, 1.0, 0.0).astype(BF)
    diagonal = jnp.where(iota((ROWS, width), 0) == iota((ROWS, width), 1) % ROWS, 1.0, 0.0).astype(BF)
    wide = dot(packed[...].reshape(terms * states, LANES), widen).astype(BF)
    for t in range(terms):
        chosen = dot(pick, wide[t * states : (t + 1) * states, :]).astype(BF)
        chosen = chosen.reshape(own, ROWS, width) * diagonal[None]
        spread[t * rows : (t + 1) * rows, :] = chosen.reshape(rows, width)


def block_kernel(edge, count, own, total, *refs):
    refs = list(refs)
    pieces = [refs.pop(0) for _ in range(lax.axis_size("mpo"))]
    numbers = [refs.pop(0) for _ in range(2)]
    if edge:
        refs.pop(0)
        halo = refs.pop(0)
    two, left, right, out = (refs.pop(0) for _ in range(4))
    if edge:
        passed = refs.pop(0)
    spread, keeps, clean, lefts, rights, mixed, joined, result, wide, index, shifts, sizes, sems = refs

    blocks, states, depth, _ = two.shape
    share = pieces[0].shape[0]
    terms = share * len(pieces)
    me = lax.axis_index("mpo")
    core = lax.rem(me, 2)
    first = lax.axis_index("blk") * blocks
    mine = (me - core) * (own // 2) if edge else me * own

    def place(n):
        return core * (blocks - 1) if edge else 1 + n

    def two_copy(n):
        return pltpu.make_async_copy(two.at[place(n)], clean.at[n], sems.at[0, n])

    def left_copy(n):
        return pltpu.make_async_copy(left.at[:, place(n)], lefts.at[n], sems.at[1, n])

    def right_copy(slot):
        if not edge:
            return pltpu.make_async_copy(right.at[:, slot], rights.at[slot], sems.at[2, slot])
        if slot == 0:
            return pltpu.make_async_copy(halo, rights.at[2 * core], sems.at[2, slot])
        near = place(0) + (0 if slot == 1 else 1 - 2 * core)
        return pltpu.make_async_copy(right.at[:, near], rights.at[1 if slot == 1 else 2 - 2 * core], sems.at[2, slot])

    def index_copy():
        return pltpu.make_async_copy(wide, index, sems.at[3, 0])

    small = [
        pltpu.make_async_copy(a, b, sems.at[5, n]) for n, (a, b) in enumerate(zip(numbers, (shifts, sizes)))
    ]
    for copy in small:
        copy.start()
    two_copy(0).start()
    for slot in range(3):
        right_copy(slot).start()
    left_copy(0).start()
    for n, piece in enumerate(pieces):
        wide[n * share : (n + 1) * share, :] = piece[:, 0, :].astype(F32).astype(I32)
    index_copy().start()
    for n, piece in enumerate(pieces):
        spread_terms(piece, spread.at[pl.ds(n * share * own * ROWS, share * own * ROWS)], own, mine)
    for copy in small:
        copy.wait()

    def live(slot):
        j = first + place(0) - 1 + slot
        return jnp.where((j >= 0) & (j < total), sizes[jnp.clip(j, 0, total - 1)], 0)

    for slot in range(count + 2):
        keeps[slot] = jnp.where(iota((ROWS, depth), 1) < live(slot), 1.0, 0.0).astype(BF)
    two_copy(0).wait()
    for n in range(1, count):
        two_copy(n).start()
        right_copy(n + 2).start()
        left_copy(n).start()

    def apply(n, leading):
        size = live(n + 1)
        if not leading:
            two_copy(n).wait()
            right_copy(n + 2).wait()
            left_copy(n).wait()

        for h in range(depth // (2 * ROWS)):
            spans = [slice((2 * h + u) * ROWS, (2 * h + u + 1) * ROWS) for u in range(2)]
            both = []
            for s in spans:
                keep_rows = jnp.where(iota((ROWS, depth), 0) + s.start < size, 1.0, 0.0).astype(BF)
                both.append([clean[n, q, s, :] * keeps[n + 1 + shifts[q]] * keep_rows for q in range(states)])
            both = jnp.concatenate([jnp.concatenate(tiles, axis=0) for tiles in both], axis=1)
            part = dot(spread[...], both).astype(BF).reshape(terms, own, ROWS, 2 * depth)
            for u in range(2):
                mixed[:, :, spans[u], :] = part[:, :, :, u * depth : (u + 1) * depth]

        if leading:
            index_copy().wait()
            for slot in range(3):
                right_copy(slot).wait()
        slot_of = [n + 1 + shifts[mine + p] for p in range(own)]
        for t in range(terms):
            bond = index[t, states + 1]
            for p in range(own):
                joined[t, :, p * depth : (p + 1) * depth] = dot(
                    mixed[t, p], rights[slot_of[p], bond]
                ).astype(BF)

        if leading:
            left_copy(n).wait()
        row = jnp.concatenate([lefts[n, index[t, states]] for t in range(terms)], axis=1)
        summed = dot(row, joined[...].reshape(terms * depth, own * depth))
        keep_rows = jnp.where(iota((depth, depth), 0) < size, 1.0, 0.0)
        for p in range(own):
            keep = keep_rows * keeps[slot_of[p], :1, :].astype(F32)
            result[n, p] = (summed[:, p * depth : (p + 1) * depth] * keep).astype(BF)

    if edge:
        apply(0, True)
        half = own // 2
        ours = pltpu.make_async_copy(
            result.at[0, pl.ds(core * half, half)], out.at[place(0)], sems.at[0, 0]
        )
        theirs = pltpu.make_async_copy(
            result.at[0, pl.ds((1 - core) * half, half)], passed, sems.at[1, 0]
        )
        theirs.start()
        ours.start()
        theirs.wait()
        ours.wait()
    else:

        def out_copy(n):
            return pltpu.make_async_copy(result.at[n], out.at[place(n)], sems.at[4, n])

        apply(0, True)
        out_copy(0).start()

        @pl.loop(1, count)
        def _(n):
            apply(n, False)
            out_copy(n).start()

        for n in range(count):
            out_copy(n).wait()


def apply_blocks(edge, pieces, shifts, sizes, two, left, right, own, total, done=None, halo=None):
    blocks, states, depth, _ = two.shape
    terms, bonds = sum(piece.shape[0] for piece in pieces), left.shape[0]
    count = 1 if edge else blocks - 2
    slots = count + 2
    anyw = pl.BlockSpec(memory_space=pl.ANY)
    vmem = pl.BlockSpec(memory_space=pltpu.VMEM)
    near = functools.partial(pltpu.with_memory_space_constraint, memory_space=pltpu.VMEM)
    far = functools.partial(pltpu.with_memory_space_constraint, memory_space=pltpu.HBM)
    operands = [*map(near, pieces), far(shifts), far(sizes)]
    operands += [far(done), near(halo)] if edge else []
    operands += map(far, (two, left, right))
    kept = own // 2 if edge else own
    out_shapes = [jax.ShapeDtypeStruct((blocks, kept, depth, depth), BF)]
    if edge:
        out_shapes.append(jax.ShapeDtypeStruct((kept, depth, depth), BF))
    buffers = [
        (terms * own * ROWS, states * ROWS),
        (slots, ROWS, depth),
        (count, states, depth, depth),
        (count, bonds, depth, depth),
        (slots, bonds, depth, depth),
        (terms, own, depth, depth),
        (terms, depth, own * depth),
        (count, own, depth, depth),
    ]
    held = sum(2 * math.prod(shape) for shape in buffers)
    return pl.pallas_call(
        functools.partial(block_kernel, edge, count, own, total),
        out_shape=out_shapes,
        in_specs=[vmem] * len(pieces) + [anyw] * (len(operands) - len(pieces)),
        out_specs=[anyw] * len(out_shapes),
        input_output_aliases={len(pieces) + 2: 0} if edge else {},
        scratch_shapes=[
            *(pltpu.VMEM(shape, BF) for shape in buffers),
            pltpu.VMEM((terms, LANES), I32),
            pltpu.SMEM((terms, LANES), I32),
            pltpu.SMEM(shifts.shape, I32),
            pltpu.SMEM(sizes.shape, I32),
            pltpu.SemaphoreType.DMA((6, slots)),
        ],
        compiler_params=pltpu.CompilerParams(vmem_limit_bytes=min(held + SPARE_VMEM, MOST_VMEM)),
        name="edge_block" if edge else "inner_blocks",
    )(*operands)


def body(two_site, left_env, right_env, mpo_terms, term_left, term_right, shifts, block_sizes):
    blocks, states = two_site.shape[:2]
    groups, count = lax.axis_size("mpo"), lax.axis_size("blk")
    own, total = states // groups, blocks * count
    core = lax.rem(lax.axis_index("mpo"), 2)

    packed, sent = ready(term_left, term_right, mpo_terms, right_env)
    place = lambda m, b: m * count + b
    up = [(place(m, b), place(m, b + 1)) for m in range(0, groups, 2) for b in range(count - 1)]
    down = [(place(m, b + 1), place(m, b)) for m in range(1, groups, 2) for b in range(count - 1)]
    halo = lax.ppermute(sent, ("mpo", "blk"), up + down)
    pieces = gathered(packed, "mpo")

    arrays = (pieces, shifts, block_sizes, two_site, left_env, right_env)
    (done,) = apply_blocks(False, *arrays, own, total)
    done, passed = apply_blocks(True, *arrays, 2 * own, total, done, halo)
    passed = lax.ppermute(passed, "mpo", [(m, m ^ 1) for m in range(groups)])
    return lax.dynamic_update_slice(done, passed[None], ((1 - core) * (blocks - 1), 0, 0, 0))


def solution(mesh):
    return jax.shard_map(
        body,
        mesh=mesh,
        in_specs=(
            P("blk", None, None, None),
            P(None, "blk", None, None),
            P(None, "blk", None, None),
            P("mpo", None, None),
            P("mpo"),
            P("mpo"),
            P(),
            P(),
        ),
        out_specs=P("blk", "mpo", None, None),
        check_vma=False,
    )
```
